32 devices in a mesh: fsdp: 4 (over z), cb: 8 (over y, x, core).
Axes of the slice: x: 2, y: 2, z: 4, core: 2. Of those that a mesh axis runs over, the one named last changes fastest.
Arguments:
- frames_in: bfloat16 [4, 256, 6144], P('fsdp', 'cb'), may hold values from -6 to 6
- valid_len: int32 [4], P('fsdp'), may hold values from 128 to 256
- tokens: int32 [4, 8, 256], P('fsdp', 'cb'), may hold values from 0 to 2047
- t_gain: float32 [6144], replicated, may hold values from 0.25 to 1.75
- w_qkv: bfloat16 [6144, 12288], P('fsdp', 'cb'), as said below
- w_out: bfloat16 [4096, 6144], P('cb', 'fsdp'), may hold values from -0.09375 to 0.09375
- h_gain: float32 [6144], replicated, may hold values from 0.25 to 1.75
- d_in: bfloat16 [8, 6144, 1024], P('cb'), may hold values from -0.078125 to 0.078125
- d_embed: bfloat16 [8, 2048, 1024], P('cb'), may hold values from -6 to 6
- d_gain: float32 [8, 1024], P('cb'), may hold values from 0.25 to 1.75
- d_qkv: bfloat16 [8, 1024, 3072], P('cb'), as said below
Outputs:
- depth_mix: bfloat16 [4, 8, 256, 1024], P('fsdp', 'cb')
The draws below stay inside these ranges and needn't reach their ends.
Inputs may be any that keep to these rules, and one draw needn't show every extreme that they name: `w_qkv`: every entry of the temporal projections has magnitude at most 31 / sqrt(6144). `d_qkv`: every entry of the depth projections has magnitude at most 31 / sqrt(1024).
All inputs are finite; a program needn't handle non-finite values.
Results may differ from the reference program's by a relative error of at most 0.012.
Values may be sent and summed in bfloat16 or wider, within the bound.
A program may use at most 128 MiB of HBM per device.

```python
import math
import jax
import jax.numpy as jnp
import numpy as np
from jax import lax

D = 6144
HEADS = 32
HEAD = 128
LENGTH = 256
DD = 1024
DHEADS = 16
DHEAD = 64
CARD = 2048
SEQS = 4
CODEBOOKS = 8


def draw_w_qkv(key, part):
    first = jax.random.fold_in(jax.random.fold_in(key, 11), 0)
    parts = jnp.clip(jax.random.normal(first, (D, HEADS, 3, HEAD), jnp.float32), -4.0, 4.0)
    return (parts * D ** (-0.5)).reshape(D, 3 * HEADS * HEAD).astype(jnp.bfloat16)


def draw_d_qkv(key, part):
    first = jax.random.fold_in(jax.random.fold_in(key, 23), 0)
    parts = jnp.clip(jax.random.normal(first, (CODEBOOKS, DD, 3, DHEADS, DHEAD), jnp.float32), -4.0, 4.0)
    return (parts * DD ** (-0.5)).reshape(CODEBOOKS, DD, 3 * DD).astype(jnp.bfloat16)


def touch_ends(array, rng, smallest, largest):
    longest = array.shape.index(max(array.shape))
    spots = []
    for shift in (0, 1):
        where = [jax.random.randint(jax.random.fold_in(rng, axis), (), 0, length) for axis, length in enumerate(array.shape)]
        where[longest] = (where[longest] + shift) % array.shape[longest]
        spots.append(tuple(where))
    return array.at[spots[0]].set(smallest).at[spots[1]].set(largest)


def block_scale(rng, extent, cuts, low, high):
    def one(position, blocks):
        steps = jax.random.uniform(jax.random.fold_in(jax.random.fold_in(rng, 6), position), (blocks,), jnp.float32, low / len(cuts), high / len(cuts))
        return jnp.repeat(jnp.exp(steps), extent[position] // blocks).reshape((-1,) + (1,) * (len(extent) - position - 1))

    level = one(*cuts[0])
    for cut in cuts[1:]:
        level = level * one(*cut)
    return level


def rank_table(number_of, lean):
    weights = [(1 << 20) // math.isqrt(standing ** lean) + 1 for standing in range(1, number_of + 1)]
    width = 1 + sum(weights) // (1 << 30)
    return np.cumsum(np.array([max(1, weight // width) for weight in weights]))


def skewed_ids(stream_key, dims, amount, lean):
    grid = rank_table(amount, lean)
    pick = jax.random.randint(jax.random.fold_in(stream_key, 1), dims, 0, int(grid[amount - 1]))
    grade = jnp.searchsorted(jnp.asarray(grid, jnp.int32), pick, side="right")
    return jax.random.permutation(jax.random.fold_in(stream_key, 2), amount)[grade].astype(jnp.int32)


def scatter_about(own_key, shape, deviation, limit, cuts=(), held_as=jnp.bfloat16):
    values = jax.random.normal(own_key, shape, jnp.float32) * deviation
    if len(cuts) > 0:
        values = block_scale(own_key, shape, cuts, -0.22, 0.18) * values
    return jnp.clip(values, min=-limit, max=limit).astype(held_as)


def setup_inputs(seed: int = 0) -> dict:
    streams_of = jax.random.split(jax.random.key(seed), 12)
    return {
        "frames_in": scatter_about(streams_of[0], (SEQS, LENGTH, D), 1.0, 6.0, ((0, 4), (1, 8))),
        "valid_len": touch_ends(jax.random.randint(streams_of[1], (SEQS,), LENGTH // 2, LENGTH + 1), jax.random.fold_in(streams_of[1], 1), LENGTH // 2, LENGTH).astype(jnp.int32),
        "tokens": touch_ends(skewed_ids(streams_of[2], (SEQS, CODEBOOKS, LENGTH), CARD, 2), jax.random.fold_in(streams_of[2], 3), 0, CARD - 1).astype(jnp.int32),
        "t_gain": jnp.clip(1.0 + 0.15 * jax.random.normal(streams_of[3], (D,), jnp.float32), 0.25, 1.75),
        "w_qkv": draw_w_qkv(jax.random.fold_in(streams_of[11], 71), 0),
        "w_out": scatter_about(streams_of[5], (HEADS * HEAD, D), (HEADS * HEAD) ** -0.5, 0.09375, ((0, 8), (1, 4))),
        "h_gain": jnp.clip(1.0 + 0.15 * jax.random.normal(streams_of[6], (D,), jnp.float32), 0.25, 1.75),
        "d_in": scatter_about(streams_of[7], (CODEBOOKS, D, DD), D ** -0.5, 0.078125, ((0, 8),)),
        "d_embed": scatter_about(streams_of[8], (CODEBOOKS, CARD, DD), 1.0, 6.0, ((0, 8),)),
        "d_gain": jnp.clip(1.0 + 0.15 * jax.random.normal(streams_of[9], (CODEBOOKS, DD), jnp.float32), 0.25, 1.75),
        "d_qkv": draw_d_qkv(jax.random.fold_in(streams_of[11], 71), 0),
    }


EPS = 1e-05
NEG = -1e+30

def rms_scale(values, gain):
    mean_sq = lax.optimization_barrier(jnp.mean(values * values, axis=-1, keepdims=True))
    return values * lax.rsqrt(mean_sq + EPS) * gain

def reference(frames_in, valid_len, tokens, t_gain, w_qkv, w_out, h_gain, d_in, d_embed, d_gain, d_qkv):
    base = frames_in.astype(jnp.float32)
    normed = rms_scale(base, t_gain).astype(jnp.bfloat16)
    packed = jnp.dot(normed.reshape(SEQS * LENGTH, D), w_qkv, preferred_element_type=jnp.float32).astype(jnp.bfloat16)
    packed = packed.reshape(SEQS, LENGTH, HEADS, 3, HEAD).astype(jnp.float32)
    query = packed[:, :, :, 0]
    keys = packed[:, :, :, 1]
    values = packed[:, :, :, 2]
    scores = jnp.einsum('sihe,sjhe->shij', query, keys) / math.sqrt(HEAD)
    rows = jnp.arange(LENGTH, dtype=jnp.int32)[:, None]
    cols = jnp.arange(LENGTH, dtype=jnp.int32)[None, :]
    allowed = (cols <= rows)[None, None] & (cols[None, None] < valid_len[:, None, None, None])
    scores = jnp.where(allowed, scores, NEG)
    top = lax.optimization_barrier(jnp.max(scores, axis=-1, keepdims=True))
    expo = jnp.where(allowed, jnp.exp(scores - top), 0.0)
    probs = (expo / lax.optimization_barrier(jnp.sum(expo, axis=-1, keepdims=True))).astype(jnp.bfloat16)
    mixed = jnp.einsum('shij,sjhe->sihe', probs.astype(jnp.float32), values).astype(jnp.bfloat16)
    proj = jnp.dot(mixed.reshape(SEQS * LENGTH, HEADS * HEAD), w_out, preferred_element_type=jnp.float32)
    hidden = base + proj.reshape(SEQS, LENGTH, D)
    hnorm = rms_scale(hidden, h_gain).astype(jnp.bfloat16).reshape(SEQS * LENGTH, D)

    def section(inputs):
        weight_in, table, gain, weight_qkv, ids = inputs
        lifted = jnp.dot(hnorm, weight_in, preferred_element_type=jnp.float32).reshape(SEQS, LENGTH, DD)
        lifted = lifted + jnp.take(table, ids, axis=0).astype(jnp.float32)
        dnorm = rms_scale(lifted, gain).astype(jnp.bfloat16)
        result = jnp.dot(dnorm.reshape(SEQS * LENGTH, DD), weight_qkv, preferred_element_type=jnp.float32)
        return result.astype(jnp.bfloat16).reshape(SEQS, LENGTH, 3 * DD)
    dqkv = lax.map(section, (d_in, d_embed, d_gain, d_qkv, jnp.swapaxes(tokens, 0, 1)))
    dq = dqkv[..., :DD].reshape(CODEBOOKS, SEQS, LENGTH, DHEADS, DHEAD).astype(jnp.float32)
    dk = dqkv[..., DD:2 * DD].reshape(CODEBOOKS, SEQS, LENGTH, DHEADS, DHEAD).astype(jnp.float32)
    dv = dqkv[..., 2 * DD:].reshape(CODEBOOKS, SEQS, LENGTH, DHEADS, DHEAD).astype(jnp.float32)
    dscore = jnp.einsum('csihe,jsihe->sihcj', dq, dk) / math.sqrt(DHEAD)
    causal = jnp.arange(CODEBOOKS, dtype=jnp.int32)[:, None] >= jnp.arange(CODEBOOKS, dtype=jnp.int32)[None, :]
    dscore = jnp.where(causal, dscore, NEG)
    dtop = lax.optimization_barrier(jnp.max(dscore, axis=-1, keepdims=True))
    dexp = jnp.where(causal, jnp.exp(dscore - dtop), 0.0)
    dprob = dexp / lax.optimization_barrier(jnp.sum(dexp, axis=-1, keepdims=True))
    out = jnp.einsum('sihcj,jsihe->scihe', dprob, dv)
    return out.reshape(SEQS, CODEBOOKS, LENGTH, DD).astype(jnp.bfloat16)
```

```python
import functools
import math

import jax
import jax.numpy as jnp
from jax import lax
from jax.experimental import pallas as pl
from jax.experimental.pallas import tpu as pltpu
from jax.sharding import PartitionSpec as P

HEAD = 128
DHEAD = 64


EPS = 1e-05
NEG = -1e30


def rms_scale(values, gain):
    mean_sq = jnp.mean(values * values, axis=-1, keepdims=True)
    return values * lax.rsqrt(mean_sq + EPS) * gain


MESH = pl.DeviceIdType.MESH
VMEM_LIMIT = 56 * 1024 * 1024


def entry_barrier(seqs, chips, f, chip, core):
    barrier = pltpu.get_barrier_semaphore()
    for d in range(1, seqs):
        pl.semaphore_signal(barrier, inc=1, device_id={"fsdp": lax.rem(f + d, seqs)}, device_id_type=MESH)
    for e in range(1, chips):
        peer = lax.rem(chip + e, chips) * 2 + core
        pl.semaphore_signal(barrier, inc=1, device_id={"cb": peer}, device_id_type=MESH)
    pl.semaphore_signal(barrier, inc=1, device_id={"cb": chip * 2 + 1 - core}, device_id_type=MESH)
    pl.semaphore_wait(barrier, seqs + chips - 1)


def send(src, dst, send_sem, recv_sem, device):
    return pltpu.make_async_remote_copy(
        src_ref=src, dst_ref=dst, send_sem=send_sem, recv_sem=recv_sem,
        device_id=device, device_id_type=MESH,
    )


def qkv_kernel(
    seqs, chips, frames, gain, w_hbm, out, normed, gat, w, part, from_left, from_right,
    z_send, z_recv, c_send, c_recv, b_send, b_recv, right_send, right_recv, left_send, left_recv, w_sem,
):
    f = lax.axis_index("fsdp")
    me = lax.axis_index("cb")
    chip, core = lax.div(me, 2), lax.rem(me, 2)
    sibling = chip * 2 + 1 - core
    few, wide = frames.shape
    width = wide // seqs
    length = out.shape[0]
    cols = out.shape[1]
    last = seqs - 1
    order = []
    for k in range(seqs):
        order.append(last - k // 2 if k % 2 == 0 else k // 2)

    load = pltpu.make_async_copy(w_hbm, w, w_sem)
    load.start()
    entry_barrier(seqs, chips, f, chip, core)
    total = jnp.zeros((few, 1), jnp.float32)
    for b in range(seqs):
        block = frames[:, b * width : (b + 1) * width].astype(jnp.float32)
        total = total + jnp.sum(block * block, axis=-1, keepdims=True)
    scale = lax.rsqrt(total / wide + EPS)
    for b in range(seqs):
        block = frames[:, b * width : (b + 1) * width].astype(jnp.float32)
        normed[b] = (block * scale * gain[:, b * width : (b + 1) * width]).astype(jnp.bfloat16)
    gat[me, f] = normed[f]

    def along_z(t):
        return send(normed.at[t], gat.at[me, f], z_send.at[t], z_recv.at[f], {"fsdp": t})

    for t in order:
        @pl.when(t != f)
        def _():
            along_z(t).start()

    def to_chip(s, e):
        peer = lax.rem(chip + e, chips) * 2 + core
        return send(gat.at[me, s], gat.at[me, s], c_send.at[s, e], c_recv.at[s, e], {"cb": peer})

    def to_sibling(s, e):
        source = lax.rem(chip - e + chips, chips) * 2 + core
        return send(gat.at[source, s], gat.at[source, s], b_send.at[s, e], b_recv.at[s, e], {"cb": sibling})

    for s in order:
        @pl.when(s != f)
        def _():
            send(normed.at[s], gat.at[me, s], z_send.at[s], z_recv.at[s], {"fsdp": s}).wait_recv()

        for e in range(1, chips):
            to_chip(s, e).start()
        to_sibling(s, 0).start()

    def to_right(t):
        return send(part.at[t], from_left.at[t], right_send.at[t], right_recv.at[t], {"fsdp": lax.rem(f + 1, seqs)})

    def to_left(t):
        return send(part.at[t], from_right.at[t], left_send.at[t], left_recv.at[t], {"fsdp": lax.rem(f + last, seqs)})

    load.wait()
    tile = 256
    for s in order:
        for e in range(1, chips):
            source = lax.rem(chip - e + chips, chips) * 2 + core
            send(gat.at[source, s], gat.at[source, s], c_send.at[s, e], c_recv.at[s, e], {"cb": sibling}).wait_recv()
            to_sibling(s, e).start()
        for e in range(chips):
            source = lax.rem(chip - e + chips, chips) * 2 + 1 - core
            send(gat.at[source, s], gat.at[source, s], b_send.at[s, e], b_recv.at[s, e], {"cb": sibling}).wait_recv()

        def multiply(step, carry):
            at = pl.ds(pl.multiple_of(step * tile, tile), tile)
            lhs = gat[:, s].reshape(length, width)
            part[s, :, at] = jnp.dot(lhs, w[:, at], preferred_element_type=jnp.float32).astype(jnp.bfloat16)
            return carry

        lax.fori_loop(0, cols // tile, multiply, 0)
        if s > 0:
            @pl.when(f == 0)
            def _():
                to_right(s).start()
        if s < last:
            @pl.when(f == last)
            def _():
                to_left(s).start()

    def add(target, t, other):
        def rows(step, carry):
            at = pl.ds(pl.multiple_of(step * 32, 32), 32)
            target[t, at] = (target[t, at].astype(jnp.float32) + other[t, at].astype(jnp.float32)).astype(jnp.bfloat16)
            return carry

        lax.fori_loop(0, length // 32, rows, 0)

    for k in range(1, seqs):
        t = seqs - k

        @pl.when((f > 0) & (t > f))
        def _():
            to_right(t).wait_recv()
            add(part, t, from_left)
            to_right(t).start()

        u = k - 1

        @pl.when((f < last) & (u < f))
        def _():
            to_left(u).wait_recv()
            add(part, u, from_right)
            to_left(u).start()

    @pl.when(f > 0)
    def _():
        to_right(f).wait_recv()
        add(part, f, from_left)

    @pl.when(f < last)
    def _():
        to_left(f).wait_recv()
        add(part, f, from_right)

    def finish(step, carry):
        at = pl.ds(pl.multiple_of(step * 32, 32), 32)
        out[at] = part[f, at]
        return carry

    lax.fori_loop(0, length // 32, finish, 0)

    for s in range(seqs):
        @pl.when(s != f)
        def _():
            along_z(s).wait_send()

        @pl.when(s > f)
        def _():
            to_right(s).wait_send()

        @pl.when(s < f)
        def _():
            to_left(s).wait_send()

        for e in range(chips):
            to_sibling(s, e).wait_send()
            if e > 0:
                to_chip(s, e).wait_send()


def temporal_qkv(seqs, parts, own, gain, w_qkv):
    few, wide = own.shape
    width, cols = w_qkv.shape
    chips = parts // 2
    length = parts * few
    dma = pltpu.SemaphoreType.DMA
    vmem = pl.BlockSpec(memory_space=pltpu.VMEM)
    return pl.pallas_call(
        functools.partial(qkv_kernel, seqs, chips),
        out_shape=jax.ShapeDtypeStruct((length, cols), jnp.bfloat16),
        in_specs=[vmem, vmem, pl.BlockSpec(memory_space=pl.ANY)],
        out_specs=vmem,
        scratch_shapes=[
            pltpu.VMEM((seqs, few, width), jnp.bfloat16),
            pltpu.VMEM((parts, seqs, few, width), jnp.bfloat16),
            pltpu.VMEM((width, cols), jnp.bfloat16),
            pltpu.VMEM((seqs, length, cols), jnp.bfloat16),
            pltpu.VMEM((seqs, length, cols), jnp.bfloat16),
            pltpu.VMEM((seqs, length, cols), jnp.bfloat16),
            dma((seqs,)), dma((seqs,)),
            dma((seqs, chips)), dma((seqs, chips)),
            dma((seqs, chips)), dma((seqs, chips)),
            dma((seqs,)), dma((seqs,)), dma((seqs,)), dma((seqs,)),
            dma,
        ],
        compiler_params=pltpu.CompilerParams(
            collective_id=0, has_side_effects=True, vmem_limit_bytes=VMEM_LIMIT
        ),
        cost_estimate=pl.CostEstimate(
            flops=2 * seqs * length * width * cols, bytes_accessed=2 * width * cols, transcendentals=0
        ),
    )(own, gain, w_qkv)


def out_kernel(
    seqs, chips, mixed, w, own, gain, out, gath, part, from_sib, acc, from_chip, total, cols, hid, gat,
    z_send, z_recv, s_send, s_recv, c_send, c_recv, t_send, t_recv, g_send, g_recv, b_send, b_recv, o_sem,
):
    f = lax.axis_index("fsdp")
    me = lax.axis_index("cb")
    chip, core = lax.div(me, 2), lax.rem(me, 2)
    sibling = chip * 2 + 1 - core
    few, wide = own.shape
    width = wide // seqs
    length = mixed.shape[0]
    tile = 256
    entry_barrier(seqs, chips, f, chip, core)

    def along_z(d):
        return send(mixed, gath.at[f], z_send.at[d], z_recv.at[d], {"fsdp": lax.rem(f + d, seqs)})

    for d in range(1, seqs):
        along_z(d).start()
    gath[f] = mixed[...]

    def to_sibling(s, d):
        return send(part.at[1 - core, s], from_sib.at[s], s_send.at[d], s_recv.at[d], {"cb": sibling})

    def to_chip(s, d, e):
        q = lax.rem(chip + e, chips)
        return send(acc.at[s, q], from_chip.at[s, e], c_send.at[d, e], c_recv.at[d, e], {"cb": q * 2 + core})

    def to_seq(s, d):
        return send(total.at[s], cols.at[f], t_send.at[d], t_recv.at[d], {"fsdp": s})

    for d in range(seqs):
        s = lax.rem(f - d + seqs, seqs)
        if d > 0:
            along_z(d).wait_recv()

        def multiply(step, carry):
            at = pl.ds(pl.multiple_of(step * tile, tile), tile)
            value = jnp.dot(gath[s], w[:, at], preferred_element_type=jnp.float32).astype(jnp.bfloat16)
            value = value.reshape(chips, 2, few, tile)
            part[0, s, :, :, at] = value[:, 0]
            part[1, s, :, :, at] = value[:, 1]
            return carry

        lax.fori_loop(0, width // tile, multiply, 0)
        to_sibling(s, d).start()

    for d in range(seqs):
        s = lax.rem(f - d + seqs, seqs)
        to_sibling(s, d).wait_recv()

        def pair(q, carry):
            acc[s, q] = (
                part[core, s, q].astype(jnp.float32) + from_sib[s, q].astype(jnp.float32)
            ).astype(jnp.bfloat16)
            return carry

        lax.fori_loop(0, chips, pair, 0)
        for e in range(1, chips):
            to_chip(s, d, e).start()

    for d in range(seqs):
        s = lax.rem(f - d + seqs, seqs)
        value = acc[s, chip].astype(jnp.float32)
        for e in range(1, chips):
            to_chip(s, d, e).wait_recv()
            value = value + from_chip[s, e].astype(jnp.float32)
        if d > 0:
            total[s] = value.astype(jnp.bfloat16)
            to_seq(s, d).start()
        else:
            cols[f] = value.astype(jnp.bfloat16)

    for d in range(1, seqs):
        to_seq(lax.rem(f - d + seqs, seqs), d).wait_recv()
    square = jnp.zeros((few, 1), jnp.float32)
    for b in range(seqs):
        at = slice(b * width, (b + 1) * width)
        block = own[:, at].astype(jnp.float32) + cols[b].astype(jnp.float32)
        hid[:, at] = block
        square = square + jnp.sum(block * block, axis=-1, keepdims=True)
    scale = lax.rsqrt(square / wide + EPS)
    for b in range(seqs):
        at = slice(b * width, (b + 1) * width)
        gat[me, :, at] = (hid[:, at] * scale * gain[:, at]).astype(jnp.bfloat16)

    def share(e):
        peer = lax.rem(chip + e, chips) * 2 + core
        return send(gat.at[me], gat.at[me], g_send.at[e], g_recv.at[e], {"cb": peer})

    def forward(e):
        source = lax.rem(chip - e + chips, chips) * 2 + core
        return send(gat.at[source], gat.at[source], b_send.at[e], b_recv.at[e], {"cb": sibling})

    for e in range(1, chips):
        share(e).start()
    forward(0).start()
    for e in range(1, chips):
        share(e).wait_recv()
        forward(e).start()
    for e in range(chips):
        forward(e).wait_recv()
    keep = pltpu.make_async_copy(gat, out, o_sem)
    keep.start()
    for d in range(seqs):
        s = lax.rem(f - d + seqs, seqs)
        to_sibling(s, d).wait_send()
        for e in range(1, chips):
            to_chip(s, d, e).wait_send()
        if d > 0:
            along_z(d).wait_send()
            to_seq(s, d).wait_send()
    for e in range(chips):
        forward(e).wait_send()
        if e > 0:
            share(e).wait_send()
    keep.wait()


def temporal_out(seqs, parts, mixed, w_out, own, gain):
    few, wide = own.shape
    depth, width = w_out.shape
    chips = parts // 2
    length = parts * few
    dma = pltpu.SemaphoreType.DMA
    vmem = pl.BlockSpec(memory_space=pltpu.VMEM)
    bf16 = jnp.bfloat16
    return pl.pallas_call(
        functools.partial(out_kernel, seqs, chips),
        out_shape=jax.ShapeDtypeStruct((parts, few, wide), bf16),
        in_specs=[vmem] * 4,
        out_specs=pl.BlockSpec(memory_space=pl.ANY),
        scratch_shapes=[
            pltpu.VMEM((seqs, length, depth), bf16),
            pltpu.VMEM((2, seqs, chips, few, width), bf16),
            pltpu.VMEM((seqs, chips, few, width), bf16),
            pltpu.VMEM((seqs, chips, few, width), bf16),
            pltpu.VMEM((seqs, chips, few, width), bf16),
            pltpu.VMEM((seqs, few, width), bf16),
            pltpu.VMEM((seqs, few, width), bf16),
            pltpu.VMEM((few, wide), jnp.float32),
            pltpu.VMEM((parts, few, wide), bf16),
            dma((seqs,)), dma((seqs,)),
            dma((seqs,)), dma((seqs,)),
            dma((seqs, chips)), dma((seqs, chips)),
            dma((seqs,)), dma((seqs,)),
            dma((chips,)), dma((chips,)),
            dma((chips,)), dma((chips,)),
            dma,
        ],
        compiler_params=pltpu.CompilerParams(
            collective_id=1, has_side_effects=True, vmem_limit_bytes=VMEM_LIMIT
        ),
        cost_estimate=pl.CostEstimate(
            flops=2 * seqs * length * width * depth, bytes_accessed=2 * depth * width, transcendentals=0
        ),
    )(mixed, w_out, own, gain)


def temporal_attention(packed, valid):
    length = packed.shape[0]
    packed = packed.reshape(length, -1, 3, HEAD)
    query = packed[:, :, 0]
    keys = packed[:, :, 1]
    values = packed[:, :, 2]
    scores = jnp.einsum(
        "ihe,jhe->hij", query, keys, preferred_element_type=jnp.float32
    ) / math.sqrt(HEAD)
    rows = lax.broadcasted_iota(jnp.int32, (length, length), 0)
    cols = lax.broadcasted_iota(jnp.int32, (length, length), 1)
    allowed = ((cols <= rows) & (cols < valid))[None]
    scores = jnp.where(allowed, scores, NEG)
    top = jnp.max(scores, axis=-1, keepdims=True)
    expo = jnp.where(allowed, jnp.exp(scores - top), 0.0)
    probs = (expo / jnp.sum(expo, axis=-1, keepdims=True)).astype(jnp.bfloat16)
    mixed = jnp.einsum("hij,jhe->ihe", probs, values, preferred_element_type=jnp.float32)
    return mixed.astype(jnp.bfloat16).reshape(length, -1)


def depth_attention(qkv):
    count, frames, width = qkv.shape
    inner = width // 3
    heads = inner // DHEAD
    query = qkv[:, :, :inner].astype(jnp.float32)
    keys = qkv[:, :, inner : 2 * inner].astype(jnp.float32)
    values = qkv[:, :, 2 * inner :].astype(jnp.float32)
    lane = lax.broadcasted_iota(jnp.int32, (inner, heads), 0) // DHEAD
    head = lax.broadcasted_iota(jnp.int32, (inner, heads), 1)
    seg = (lane == head).astype(jnp.bfloat16)
    prod = (query[:, None] * keys[None]).astype(jnp.bfloat16)
    score = jnp.einsum(
        "cnix,xh->cnih", prod, seg, preferred_element_type=jnp.float32
    ) / math.sqrt(DHEAD)
    mine = lax.broadcasted_iota(jnp.int32, (count, count, 1, 1), 0)
    other = lax.broadcasted_iota(jnp.int32, (count, count, 1, 1), 1)
    keep = other <= mine
    score = jnp.where(keep, score, NEG)
    top = jnp.max(score, axis=1, keepdims=True)
    expo = jnp.where(keep, jnp.exp(score - top), 0.0)
    probs = (expo / jnp.sum(expo, axis=1, keepdims=True)).astype(jnp.bfloat16)
    wide = jnp.einsum("cnih,xh->cnix", probs, seg, preferred_element_type=jnp.float32)
    return jnp.sum(wide * values[None], axis=1).astype(jnp.bfloat16)


def body(frames_in, valid_len, tokens, t_gain, w_qkv, w_out, h_gain, d_in, d_embed, d_gain, d_qkv):
    seqs = lax.axis_size("fsdp")
    parts = lax.axis_size("cb")
    own = frames_in[0]
    few = own.shape[0]
    packed = temporal_qkv(seqs, parts, own, t_gain[None], w_qkv)
    mixed = temporal_attention(packed, valid_len[0])
    hnorm = temporal_out(seqs, parts, mixed, w_out, own, h_gain[None])
    hnorm = hnorm.reshape(parts * few, -1)
    lifted = jnp.dot(hnorm, d_in[0], preferred_element_type=jnp.float32)
    lifted = lifted + jnp.take(d_embed[0], tokens[0, 0], axis=0).astype(jnp.float32)
    dnorm = rms_scale(lifted, d_gain[0]).astype(jnp.bfloat16)
    depth_all = jnp.dot(dnorm, d_qkv[0], preferred_element_type=jnp.float32).astype(jnp.bfloat16)
    depth_all = lax.all_to_all(depth_all, "cb", split_axis=0, concat_axis=0, tiled=True)
    result = depth_attention(depth_all.reshape(parts, few, -1))
    result = result.reshape(parts * few, -1)
    result = lax.all_to_all(result, "cb", split_axis=0, concat_axis=0, tiled=True)
    return result[None, None]


def solution(mesh):
    placed = (
        P("fsdp", "cb", None),
        P("fsdp"),
        P("fsdp", "cb", None),
        P(),
        P("fsdp", "cb"),
        P("cb", "fsdp"),
        P(),
        P("cb", None, None),
        P("cb", None, None),
        P("cb", None),
        P("cb", None, None),
    )
    return jax.shard_map(
        body, mesh=mesh, in_specs=placed, out_specs=P("fsdp", "cb", None, None), check_vma=False
    )
```

```python
import functools
import math

import jax
import jax.numpy as jnp
from jax import lax
from jax.experimental import pallas as pl
from jax.experimental.pallas import tpu as pltpu
from jax.sharding import PartitionSpec as P

HEAD = 128
DHEAD = 64


EPS = 1e-05
NEG = -1e30


MESH = pl.DeviceIdType.MESH
VMEM_LIMIT = 56 * 1024 * 1024


def full_barrier(seqs, parts, f, me):
    barrier = pltpu.get_barrier_semaphore()
    for d in range(1, seqs):
        pl.semaphore_signal(barrier, inc=1, device_id={"fsdp": lax.rem(f + d, seqs)}, device_id_type=MESH)
    for e in range(1, parts):
        pl.semaphore_signal(barrier, inc=1, device_id={"cb": lax.rem(me + e, parts)}, device_id_type=MESH)
    pl.semaphore_wait(barrier, seqs + parts - 2)


def entry_barrier(seqs, chips, f, chip, core):
    barrier = pltpu.get_barrier_semaphore()
    for d in range(1, seqs):
        pl.semaphore_signal(barrier, inc=1, device_id={"fsdp": lax.rem(f + d, seqs)}, device_id_type=MESH)
    for e in range(1, chips):
        peer = lax.rem(chip + e, chips) * 2 + core
        pl.semaphore_signal(barrier, inc=1, device_id={"cb": peer}, device_id_type=MESH)
    pl.semaphore_signal(barrier, inc=1, device_id={"cb": chip * 2 + 1 - core}, device_id_type=MESH)
    pl.semaphore_wait(barrier, seqs + chips - 1)


def send(src, dst, send_sem, recv_sem, device):
    return pltpu.make_async_remote_copy(
        src_ref=src, dst_ref=dst, send_sem=send_sem, recv_sem=recv_sem,
        device_id=device, device_id_type=MESH,
    )


def qkv_kernel(
    seqs, chips, frames, gain, w_hbm, out, normed, gat, w, part, from_left, from_right,
    z_send, z_recv, c_send, c_recv, b_send, b_recv, right_send, right_recv, left_send, left_recv, w_sem,
):
    f = lax.axis_index("fsdp")
    me = lax.axis_index("cb")
    chip, core = lax.div(me, 2), lax.rem(me, 2)
    sibling = chip * 2 + 1 - core
    few, wide = frames.shape
    width = wide // seqs
    length = out.shape[0]
    cols = out.shape[1]
    last = seqs - 1
    order = []
    for k in range(seqs):
        order.append(last - k // 2 if k % 2 == 0 else k // 2)

    load = pltpu.make_async_copy(w_hbm, w, w_sem)
    load.start()
    entry_barrier(seqs, chips, f, chip, core)
    total = jnp.zeros((few, 1), jnp.float32)
    for b in range(seqs):
        block = frames[:, b * width : (b + 1) * width].astype(jnp.float32)
        total = total + jnp.sum(block * block, axis=-1, keepdims=True)
    scale = lax.rsqrt(total / wide + EPS)
    for b in range(seqs):
        block = frames[:, b * width : (b + 1) * width].astype(jnp.float32)
        normed[b] = (block * scale * gain[:, b * width : (b + 1) * width]).astype(jnp.bfloat16)
    gat[me, f] = normed[f]

    def along_z(t):
        return send(normed.at[t], gat.at[me, f], z_send.at[t], z_recv.at[f], {"fsdp": t})

    for t in order:
        @pl.when(t != f)
        def _():
            along_z(t).start()

    def to_chip(s, e):
        peer = lax.rem(chip + e, chips) * 2 + core
        return send(gat.at[me, s], gat.at[me, s], c_send.at[s, e], c_recv.at[s, e], {"cb": peer})

    def to_sibling(s, e):
        source = lax.rem(chip - e + chips, chips) * 2 + core
        return send(gat.at[source, s], gat.at[source, s], b_send.at[s, e], b_recv.at[s, e], {"cb": sibling})

    def push(s):
        @pl.when(s != f)
        def _():
            send(normed.at[s], gat.at[me, s], z_send.at[s], z_recv.at[s], {"fsdp": s}).wait_recv()

        for e in range(1, chips):
            to_chip(s, e).start()
        to_sibling(s, 0).start()

    push(order[0])

    def to_right(t):
        return send(part.at[t], from_left.at[t], right_send.at[t], right_recv.at[t], {"fsdp": lax.rem(f + 1, seqs)})

    def to_left(t):
        return send(part.at[t], from_right.at[t], left_send.at[t], left_recv.at[t], {"fsdp": lax.rem(f + last, seqs)})

    tile = 256
    for k, s in enumerate(order):
        if k + 1 < seqs:
            for e in range(1, chips):
                to_chip(s, e).wait_send()
            push(order[k + 1])
        for e in range(1, chips):
            source = lax.rem(chip - e + chips, chips) * 2 + core
            send(gat.at[source, s], gat.at[source, s], c_send.at[s, e], c_recv.at[s, e], {"cb": sibling}).wait_recv()
            to_sibling(s, e).start()
        for e in range(chips):
            source = lax.rem(chip - e + chips, chips) * 2 + 1 - core
            send(gat.at[source, s], gat.at[source, s], b_send.at[s, e], b_recv.at[s, e], {"cb": sibling}).wait_recv()

        if k == 0:
            load.wait()

        def multiply(step, carry):
            at = pl.ds(pl.multiple_of(step * tile, tile), tile)
            lhs = gat[:, s].reshape(length, width)
            part[s, :, at] = jnp.dot(lhs, w[:, at], preferred_element_type=jnp.float32).astype(jnp.bfloat16)
            return carry

        lax.fori_loop(0, cols // tile, multiply, 0)
        if s == last:
            @pl.when(f == 0)
            def _():
                to_right(s).start()
        if s == 0:
            @pl.when(f == last)
            def _():
                to_left(s).start()

    @pl.when(f == 0)
    def _():
        for t in range(last - 1, 0, -1):
            to_right(t + 1).wait_send()
            to_right(t).start()

    @pl.when(f == last)
    def _():
        for u in range(1, last):
            to_left(u - 1).wait_send()
            to_left(u).start()

    def add(target, t, other):
        def rows(step, carry):
            at = pl.ds(pl.multiple_of(step * 32, 32), 32)
            target[t, at] = (target[t, at].astype(jnp.float32) + other[t, at].astype(jnp.float32)).astype(jnp.bfloat16)
            return carry

        lax.fori_loop(0, length // 32, rows, 0)

    for k in range(1, seqs):
        t = seqs - k

        @pl.when((f > 0) & (t > f))
        def _():
            to_right(t).wait_recv()
            add(part, t, from_left)
            to_right(t).start()

        u = k - 1

        @pl.when((f < last) & (u < f))
        def _():
            to_left(u).wait_recv()
            add(part, u, from_right)
            to_left(u).start()

    @pl.when(f > 0)
    def _():
        to_right(f).wait_recv()
        add(part, f, from_left)

    @pl.when(f < last)
    def _():
        to_left(f).wait_recv()
        add(part, f, from_right)

    def finish(step, carry):
        at = pl.ds(pl.multiple_of(step * 32, 32), 32)
        out[at] = part[f, at]
        return carry

    lax.fori_loop(0, length // 32, finish, 0)

    for s in range(seqs):
        @pl.when(s != f)
        def _():
            along_z(s).wait_send()

        @pl.when((s > f) & ((f > 0) | (s == 1)))
        def _():
            to_right(s).wait_send()

        @pl.when((s < f) & ((f < last) | (s == last - 1)))
        def _():
            to_left(s).wait_send()

        for e in range(chips):
            to_sibling(s, e).wait_send()
            if e > 0 and s == order[-1]:
                to_chip(s, e).wait_send()


def temporal_qkv(seqs, parts, own, gain, w_qkv):
    few, wide = own.shape
    width, cols = w_qkv.shape
    chips = parts // 2
    length = parts * few
    dma = pltpu.SemaphoreType.DMA
    vmem = pl.BlockSpec(memory_space=pltpu.VMEM)
    return pl.pallas_call(
        functools.partial(qkv_kernel, seqs, chips),
        out_shape=jax.ShapeDtypeStruct((length, cols), jnp.bfloat16),
        in_specs=[vmem, vmem, pl.BlockSpec(memory_space=pl.ANY)],
        out_specs=vmem,
        scratch_shapes=[
            pltpu.VMEM((seqs, few, width), jnp.bfloat16),
            pltpu.VMEM((parts, seqs, few, width), jnp.bfloat16),
            pltpu.VMEM((width, cols), jnp.bfloat16),
            pltpu.VMEM((seqs, length, cols), jnp.bfloat16),
            pltpu.VMEM((seqs, length, cols), jnp.bfloat16),
            pltpu.VMEM((seqs, length, cols), jnp.bfloat16),
            dma((seqs,)), dma((seqs,)),
            dma((seqs, chips)), dma((seqs, chips)),
            dma((seqs, chips)), dma((seqs, chips)),
            dma((seqs,)), dma((seqs,)), dma((seqs,)), dma((seqs,)),
            dma,
        ],
        compiler_params=pltpu.CompilerParams(
            collective_id=0, has_side_effects=True, vmem_limit_bytes=VMEM_LIMIT
        ),
        cost_estimate=pl.CostEstimate(
            flops=2 * seqs * length * width * cols, bytes_accessed=2 * width * cols, transcendentals=0
        ),
    )(own, gain, w_qkv)


def out_kernel(
    seqs, chips, mixed, w, own, gain, ids, d_gain, d_in_hbm, table_hbm, d_qkv_hbm, out,
    gath, part, from_sib, acc, from_chip, total, cols, hid, gat, d_in, table, d_qkv, lifted, dnorm, mine, theirs,
    done, back,
    z_send, z_recv, s_send, s_recv, c_send, c_recv, t_send, t_recv, g_send, g_recv, b_send, b_recv,
    a_send, a_recv, r_send, r_recv, w_sem,
):
    f = lax.axis_index("fsdp")
    me = lax.axis_index("cb")
    chip, core = lax.div(me, 2), lax.rem(me, 2)
    sibling = chip * 2 + 1 - core
    few, wide = own.shape
    width = wide // seqs
    length = mixed.shape[0]
    tile = 256
    parts = 2 * chips
    inner = lifted.shape[1]
    loads = [
        pltpu.make_async_copy(table_hbm, table, w_sem.at[0]),
        pltpu.make_async_copy(d_in_hbm, d_in, w_sem.at[1]),
        pltpu.make_async_copy(d_qkv_hbm, d_qkv, w_sem.at[2]),
    ]
    for load in loads:
        load.start()
    full_barrier(seqs, parts, f, me)

    def along_z(d):
        return send(mixed, gath.at[f], z_send.at[d], z_recv.at[d], {"fsdp": lax.rem(f + d, seqs)})

    for d in range(1, seqs):
        along_z(d).start()
    gath[f] = mixed[...]

    def to_sibling(s, d):
        return send(part.at[1 - core, s], from_sib.at[s], s_send.at[d], s_recv.at[d], {"cb": sibling})

    def to_chip(s, d, e):
        q = lax.rem(chip + e, chips)
        return send(acc.at[s, q], from_chip.at[s, e], c_send.at[d, e], c_recv.at[d, e], {"cb": q * 2 + core})

    def to_seq(s, d):
        return send(total.at[s], cols.at[f], t_send.at[d], t_recv.at[d], {"fsdp": s})

    for d in range(seqs):
        s = lax.rem(f - d + seqs, seqs)
        if d > 0:
            along_z(d).wait_recv()

        def multiply(step, carry):
            at = pl.ds(pl.multiple_of(step * tile, tile), tile)
            value = jnp.dot(gath[s], w[:, at], preferred_element_type=jnp.float32).astype(jnp.bfloat16)
            value = value.reshape(chips, 2, few, tile)
            part[0, s, :, :, at] = value[:, 0]
            part[1, s, :, :, at] = value[:, 1]
            return carry

        lax.fori_loop(0, width // tile, multiply, 0)
        to_sibling(s, d).start()

    loads[0].wait()
    entries = table.shape[0]

    def lookup_tile(step, carry):
        at = pl.ds(pl.multiple_of(step * tile, tile), tile)
        spread = lax.broadcasted_iota(jnp.int32, (length, entries), 1)
        hot = jnp.where(spread == ids[...], 1.0, 0.0).astype(jnp.bfloat16)
        lifted[:, at] = jnp.dot(hot, table[:, at], preferred_element_type=jnp.float32)
        return carry

    turns = list(range(1, seqs)) + [0]

    def reduce_pair(d):
        s = lax.rem(f - d + seqs, seqs)
        to_sibling(s, d).wait_recv()

        def pair(q, carry):
            acc[s, q] = (
                part[core, s, q].astype(jnp.float32) + from_sib[s, q].astype(jnp.float32)
            ).astype(jnp.bfloat16)
            return carry

        lax.fori_loop(0, chips, pair, 0)
        for e in range(1, chips):
            to_chip(s, d, e).start()

    reduce_pair(turns[0])
    for k, d in enumerate(turns):
        s = lax.rem(f - d + seqs, seqs)
        if k + 1 < seqs:
            for e in range(1, chips):
                to_chip(s, d, e).wait_send()
            reduce_pair(turns[k + 1])
        else:
            lax.fori_loop(0, inner // tile, lookup_tile, 0)
        value = acc[s, chip].astype(jnp.float32)
        for e in range(1, chips):
            to_chip(s, d, e).wait_recv()
            value = value + from_chip[s, e].astype(jnp.float32)
        if d > 0:
            total[s] = value.astype(jnp.bfloat16)
            to_seq(s, d).start()
        else:
            cols[f] = value.astype(jnp.bfloat16)

    for d in range(1, seqs):
        to_seq(lax.rem(f - d + seqs, seqs), d).wait_recv()
    square = jnp.zeros((few, 1), jnp.float32)
    for b in range(seqs):
        at = slice(b * width, (b + 1) * width)
        block = own[:, at].astype(jnp.float32) + cols[b].astype(jnp.float32)
        hid[:, at] = block
        square = square + jnp.sum(block * block, axis=-1, keepdims=True)
    scale = lax.rsqrt(square / wide + EPS)
    for b in range(seqs):
        at = slice(b * width, (b + 1) * width)
        gat[me, :, at] = (hid[:, at] * scale * gain[:, at]).astype(jnp.bfloat16)

    def share(e):
        peer = lax.rem(chip + e, chips) * 2 + core
        return send(gat.at[me], gat.at[me], g_send.at[e], g_recv.at[e], {"cb": peer})

    def forward(e):
        source = lax.rem(chip - e + chips, chips) * 2 + core
        return send(gat.at[source], gat.at[source], b_send.at[e], b_recv.at[e], {"cb": sibling})

    for e in range(1, chips):
        share(e).start()
    forward(0).start()
    for e in range(1, chips):
        share(e).wait_recv()
        forward(e).start()
    for e in range(chips):
        forward(e).wait_recv()
    loads[1].wait()

    def lift(step, carry):
        at = pl.ds(pl.multiple_of(step * tile, tile), tile)
        lifted[:, at] += jnp.dot(gat[...].reshape(length, wide), d_in[:, at], preferred_element_type=jnp.float32)
        return carry

    lax.fori_loop(0, inner // tile, lift, 0)

    def norm_rows(step, carry):
        at = pl.ds(pl.multiple_of(step * 32, 32), 32)
        rows = lifted[at]
        mean = jnp.sum(rows * rows, axis=-1, keepdims=True) / inner
        dnorm[at] = (rows * lax.rsqrt(mean + EPS) * d_gain[...]).astype(jnp.bfloat16)
        return carry

    lax.fori_loop(0, length // 32, norm_rows, 0)

    def scatter(third, e):
        to = lax.rem(me + e, parts)
        return send(mine.at[third, to], theirs.at[third, me], a_send.at[third, e], a_recv.at[third, e], {"cb": to})

    loads[2].wait()
    for third in range(3):
        def project(step, carry):
            at = pl.ds(pl.multiple_of(step * tile, tile), tile)
            source = pl.ds(pl.multiple_of(third * inner + step * tile, tile), tile)
            value = jnp.dot(dnorm[...], d_qkv[:, source], preferred_element_type=jnp.float32).astype(jnp.bfloat16)
            mine[third, :, :, at] = value.reshape(parts, few, tile)
            return carry

        lax.fori_loop(0, inner // tile, project, 0)
        for e in range(1, parts):
            scatter(third, e).start()
        theirs[third, me] = mine[third, me]
    lane = lax.broadcasted_iota(jnp.int32, (inner, 128), 0) // DHEAD
    head = lax.broadcasted_iota(jnp.int32, (inner, 128), 1)
    seg = jnp.where(lane == head, 1.0, 0.0).astype(jnp.bfloat16)
    lane = lax.broadcasted_iota(jnp.int32, (128, inner), 1) // DHEAD
    head = lax.broadcasted_iota(jnp.int32, (128, inner), 0)
    spread = jnp.where(lane == head, 1.0, 0.0).astype(jnp.bfloat16)
    for third in range(3):
        for e in range(1, parts):
            scatter(third, e).wait_recv()

    def attend(c):
        query = theirs[0, c].astype(jnp.float32)
        prod = (theirs[1].astype(jnp.float32) * query[None]).astype(jnp.bfloat16)
        score = jnp.dot(prod.reshape(length, inner), seg, preferred_element_type=jnp.float32)
        score = score.reshape(parts, few, 128) * (1.0 / math.sqrt(DHEAD))
        keep = lax.broadcasted_iota(jnp.int32, (parts, few, 128), 0) <= c
        score = jnp.where(keep, score, NEG)
        top = jnp.max(score, axis=0, keepdims=True)
        expo = jnp.where(keep, jnp.exp(score - top), 0.0)
        probs = (expo / jnp.sum(expo, axis=0, keepdims=True)).astype(jnp.bfloat16)
        full = jnp.dot(probs.reshape(length, 128), spread, preferred_element_type=jnp.float32)
        full = full.reshape(parts, few, inner) * theirs[2].astype(jnp.float32)
        return jnp.sum(full, axis=0).astype(jnp.bfloat16)

    def give(e):
        to = lax.rem(me + e, parts)
        return send(done.at[to], back.at[me], r_send.at[e], r_recv.at[e], {"cb": to})

    def each(e, carry):
        c = lax.rem(me + e, parts)
        done[c] = attend(c)
        give(e).start()
        return carry

    lax.fori_loop(1, parts, each, 0)
    back[me] = attend(me)
    for e in range(1, parts):
        give(e).wait_recv()
    out[...] = back[...]
    for e in range(1, parts):
        give(e).wait_send()
        for third in range(3):
            scatter(third, e).wait_send()
    for d in range(seqs):
        s = lax.rem(f - d + seqs, seqs)
        to_sibling(s, d).wait_send()
        if d == turns[-1]:
            for e in range(1, chips):
                to_chip(s, d, e).wait_send()
        if d > 0:
            along_z(d).wait_send()
            to_seq(s, d).wait_send()
    for e in range(chips):
        forward(e).wait_send()
        if e > 0:
            share(e).wait_send()


def out_and_depth(seqs, parts, mixed, w_out, own, gain, ids, d_gain, d_in, table, d_qkv):
    few, wide = own.shape
    depth, width = w_out.shape
    inner = d_in.shape[1]
    chips = parts // 2
    length = parts * few
    dma = pltpu.SemaphoreType.DMA
    vmem = pl.BlockSpec(memory_space=pltpu.VMEM)
    bf16 = jnp.bfloat16
    return pl.pallas_call(
        functools.partial(out_kernel, seqs, chips),
        out_shape=jax.ShapeDtypeStruct((parts, few, inner), bf16),
        in_specs=[vmem] * 6 + [pl.BlockSpec(memory_space=pl.ANY)] * 3,
        out_specs=vmem,
        scratch_shapes=[
            pltpu.VMEM((seqs, length, depth), bf16),
            pltpu.VMEM((2, seqs, chips, few, width), bf16),
            pltpu.VMEM((seqs, chips, few, width), bf16),
            pltpu.VMEM((seqs, chips, few, width), bf16),
            pltpu.VMEM((seqs, chips, few, width), bf16),
            pltpu.VMEM((seqs, few, width), bf16),
            pltpu.VMEM((seqs, few, width), bf16),
            pltpu.VMEM((few, wide), jnp.float32),
            pltpu.VMEM((parts, few, wide), bf16),
            pltpu.VMEM(d_in.shape, bf16),
            pltpu.VMEM(table.shape, bf16),
            pltpu.VMEM(d_qkv.shape, bf16),
            pltpu.VMEM((length, inner), jnp.float32),
            pltpu.VMEM((length, inner), bf16),
            pltpu.VMEM((3, parts, few, inner), bf16),
            pltpu.VMEM((3, parts, few, inner), bf16),
            pltpu.VMEM((parts, few, inner), bf16),
            pltpu.VMEM((parts, few, inner), bf16),
            dma((seqs,)), dma((seqs,)),
            dma((seqs,)), dma((seqs,)),
            dma((seqs, chips)), dma((seqs, chips)),
            dma((seqs,)), dma((seqs,)),
            dma((chips,)), dma((chips,)),
            dma((chips,)), dma((chips,)),
            dma((3, parts)), dma((3, parts)),
            dma((parts,)), dma((parts,)),
            dma((3,)),
        ],
        compiler_params=pltpu.CompilerParams(
            collective_id=1, has_side_effects=True, vmem_limit_bytes=VMEM_LIMIT
        ),
        cost_estimate=pl.CostEstimate(
            flops=2 * seqs * length * width * depth, bytes_accessed=2 * depth * width, transcendentals=0
        ),
    )(mixed, w_out, own, gain, ids, d_gain, d_in, table, d_qkv)


def temporal_attention(packed, valid):
    length = packed.shape[0]
    packed = packed.reshape(length, -1, 3, HEAD)
    query = packed[:, :, 0]
    keys = packed[:, :, 1]
    values = packed[:, :, 2]
    scores = jnp.einsum(
        "ihe,jhe->hij", query, keys, preferred_element_type=jnp.float32
    ) / math.sqrt(HEAD)
    rows = lax.broadcasted_iota(jnp.int32, (length, length), 0)
    cols = lax.broadcasted_iota(jnp.int32, (length, length), 1)
    allowed = ((cols <= rows) & (cols < valid))[None]
    scores = jnp.where(allowed, scores, NEG)
    top = jnp.max(scores, axis=-1, keepdims=True)
    expo = jnp.where(allowed, jnp.exp(scores - top), 0.0)
    probs = (expo / jnp.sum(expo, axis=-1, keepdims=True)).astype(jnp.bfloat16)
    mixed = jnp.einsum("hij,jhe->ihe", probs, values, preferred_element_type=jnp.float32)
    return mixed.astype(jnp.bfloat16).reshape(length, -1)


def body(frames_in, valid_len, tokens, t_gain, w_qkv, w_out, h_gain, d_in, d_embed, d_gain, d_qkv):
    seqs = lax.axis_size("fsdp")
    parts = lax.axis_size("cb")
    own = frames_in[0]
    few = own.shape[0]
    packed = temporal_qkv(seqs, parts, own, t_gain[None], w_qkv)
    mixed = temporal_attention(packed, valid_len[0])
    result = out_and_depth(
        seqs, parts, mixed, w_out, own, h_gain[None], tokens[0, 0][:, None], d_gain, d_in[0], d_embed[0], d_qkv[0]
    )
    result = result.reshape(parts * few, -1)
    return result[None, None]


def solution(mesh):
    placed = (
        P("fsdp", "cb", None),
        P("fsdp"),
        P("fsdp", "cb", None),
        P(),
        P("fsdp", "cb"),
        P("cb", "fsdp"),
        P(),
        P("cb", None, None),
        P("cb", None, None),
        P("cb", None),
        P("cb", None, None),
    )
    return jax.shard_map(
        body, mesh=mesh, in_specs=placed, out_specs=P("fsdp", "cb", None, None), check_vma=False
    )
```
